32 devices in a mesh: grp: 2 (over y), sec: 16 (over z, x, core).
Axes of the slice: x: 2, y: 2, z: 4, core: 2. Of those that a mesh axis runs over, the one named last changes fastest.
Arguments:
- vectors: bfloat16 [3, 64, 64, 1024], P(None, ('grp', 'sec')), parts along dimension 1, may hold values from -6 to 6
- left_env: bfloat16 [64, 64, 128], P(('grp', 'sec')), parts along dimension 0, may hold values from -0.75 to 0.75
- right_env: bfloat16 [64, 64, 128], P(('grp', 'sec')), parts along dimension 0, may hold values from -0.5 to 0.5
- target_device: int32 [64, 16, 1], P(('grp', 'sec')), parts along dimension 0, may hold values from 0 to 15; in each aligned block of 32 rows (0 to 31, 32 to 63, ..., all dimensions but the last counted through in order) at most 4 rows name the same one
- target_slot: int32 [64, 16], P(('grp', 'sec')), parts along dimension 0, may hold values from 0 to 1
Outputs:
- products: bfloat16 [3, 64, 64, 1024], P(None, ('grp', 'sec')), parts along dimension 1
The draws below stay inside these ranges and needn't reach their ends.
There are 2 independent parts, one for each index of `grp`. The reference program is written for one: setup_inputs(seed, part) draws one part's arguments, and reference() takes and returns one part's arrays. A program takes and returns all parts, laid end to end along the dimension named above; each array names one. Nothing has to cross between parts.
Inputs may be any that keep to these rules, and one draw needn't show every extreme that they name: `target_device`: among the blocks of one device no device is named more than 4 times, and in some device's blocks one device is named exactly 4 times.
All inputs are finite; a program needn't handle non-finite values.
Results may differ from the reference program's by a relative error of at most 0.0049.
Values may be sent and summed in bfloat16 or wider, within the bound.
No kernel may reach another device: no remote copies, remote signals or barrier semaphores. Data moves between devices by JAX's collectives and lax.ppermute only.
A program may use at most 128 MiB of HBM per device.

```python
import math
import jax
import jax.numpy as jnp
import numpy as np
from jax import lax

BS = 64
PAIRS = 16
TERMS = 2
VECS = 3
SEC_DEV = 2
SECTORS = 32
PEERS = 16
ROWS_DEV = 32
CAP = 4


def set_ends(entries, own_key, low, top_value):
    dims = entries.shape
    spot = [jax.random.randint(jax.random.fold_in(own_key, axis), (), 0, dims[axis]) for axis in range(len(dims))]
    entries = entries.at[tuple(spot)].set(low)
    longest = dims.index(max(dims))
    spot[longest] = (spot[longest] + 1) % dims[longest]
    return entries.at[tuple(spot)].set(top_value)


def shard_levels(key, extent, cuts, least, high):
    factor_of = 1.0
    for axis_at, blocks in cuts:
        steps = jax.random.uniform(jax.random.fold_in(jax.random.fold_in(key, 6), axis_at), (blocks,), jnp.float32, least / len(cuts), high / len(cuts))
        factor_of = factor_of * jnp.repeat(jnp.exp(steps), extent[axis_at] // blocks).reshape((-1,) + (1,) * (len(extent) - 1 - axis_at))
    return factor_of


def deal_out(rng, own, number, rows, number_of, top, bound, lean):
    order = jax.random.permutation(rng, number_of)
    heavy_load, common = portions_of(number_of, rows * top, bound, lean, True), portions_of(number_of, rows * top, bound, lean, False)
    places = jnp.arange(number_of)

    def named(tallies, turn):
        used = int((tallies > 0).sum())
        fixed = max(1, used // 4)
        moved = fixed + (places - fixed + turn * (used - fixed)) % max(1, number_of - fixed)
        return jnp.zeros((number_of,), jnp.int32).at[order[jnp.where(places < fixed, places, moved)]].set(jnp.asarray(tallies, jnp.int32))

    tallies = jnp.where(number % 4 == 0, named(heavy_load, number // 4), named(common, number - number // 4 - 1))
    mixed = jax.random.permutation(jax.random.fold_in(own, 3), number_of)
    donor, receiver = mixed[0:number_of // 2 * 2:2], mixed[1:number_of // 2 * 2:2]
    room = jnp.minimum(tallies[donor] - 1, bound - tallies[receiver]) // 2
    room = jnp.where((donor == order[0]) | (receiver == order[0]) | (tallies[receiver] == 0), 0, jnp.maximum(room, 0))
    moved = jax.random.randint(jax.random.fold_in(own, 4), (number_of // 2,), 0, 1 << 20) % (room + 1)
    tallies = tallies.at[donor].add(-moved).at[receiver].add(moved)
    items = jnp.searchsorted(jnp.cumsum(tallies), jnp.arange(rows * top), side="right").astype(jnp.int32)
    listing = items.reshape(top, rows).T
    listing = listing[jax.random.permutation(jax.random.fold_in(own, 1), rows)]
    turn = jax.random.randint(jax.random.fold_in(own, 2), (rows, 1), 0, top)
    return jnp.take_along_axis(listing, (jnp.arange(top)[None, :] + turn) % top, axis=1)


def portions_of(count, total, most, lean, full):
    portions = [(1 << 20) // math.isqrt(rank ** lean) + 1 for rank in range(1, count + 1)]
    largest = most if full else min(most, max(-(-total // count), total * portions[0] // sum(portions)))
    least = 1 if total - largest >= count - 1 else 0
    given, surplus = [largest] + [least] * (count - 1), total - largest - least * (count - 1)
    while surplus > 0:
        candidates = [i for i in range(1, count) if given[i] < largest] or [i for i in range(1, count) if given[i] < most]
        pool, remaining = sum([portions[i] for i in candidates]), surplus
        for i in candidates:
            more = min(most - given[i], max(1, remaining * portions[i] // pool), surplus)
            given[i] = given[i] + more
            surplus = surplus - more
    return np.array(given)


def scatter_about(own_key, dims, width, limit, cuts=(), dtype=jnp.bfloat16):
    values = jax.random.normal(own_key, dims, jnp.float32) * width
    if len(cuts) > 0:
        values = shard_levels(own_key, dims, cuts, -0.22, 0.18) * values
    return jnp.clip(values, min=-limit, max=limit).astype(dtype)


def setup_inputs(seed: int = 0, part: int = 0) -> dict:
    keys = jax.random.split(jax.random.key(seed), 6)
    part_keys = jax.random.split(jax.random.fold_in(keys[5], part), 6)
    vectors = scatter_about(part_keys[0], (VECS, SECTORS, BS, PAIRS * BS), 1.0, 6.0, ((1, 16),))
    left_env = scatter_about(part_keys[1], (SECTORS, BS, TERMS * BS), BS ** -0.5, 0.75, ((0, 16),))
    right_env = scatter_about(part_keys[2], (SECTORS, BS, TERMS * BS), (TERMS * BS) ** -0.5, 0.5, ((0, 16),))
    target_device_keys = jax.random.split(jax.random.fold_in(part_keys[3], 1), SECTORS * PAIRS // ROWS_DEV)
    target_device_turns = jax.random.permutation(jax.random.fold_in(part_keys[3], 3), SECTORS * PAIRS // ROWS_DEV)
    target_device = jax.vmap(lambda own, number: deal_out(jax.random.fold_in(part_keys[3], 2), own, number, ROWS_DEV, PEERS, 1, CAP, 2))(target_device_keys, target_device_turns).reshape((SECTORS, PAIRS, 1))
    target_slot = set_ends(jax.random.randint(part_keys[4], (SECTORS, PAIRS), 0, SEC_DEV), jax.random.fold_in(part_keys[4], 1), 0, SEC_DEV - 1).astype(jnp.int32)
    return {"vectors": vectors, "left_env": left_env, "right_env": right_env, "target_device": target_device, "target_slot": target_slot}


def reference(vectors, left_env, right_env, target_device, target_slot):
    sector_ids = (target_device[:, :, 0] * SEC_DEV + target_slot).astype(jnp.int32)

    def one_sector(items):
        part, left, ids = items
        lefts = left.reshape(BS, TERMS, BS).astype(jnp.float32)
        pieces = part.reshape(VECS, BS, PAIRS, BS).astype(jnp.float32)
        mixed = jnp.einsum('mwi,vmpj->pviwj', lefts, pieces).astype(jnp.bfloat16)
        mixed = mixed.reshape(PAIRS, VECS, BS, TERMS * BS)
        chosen = jnp.take(right_env, ids, axis=0)
        result = jnp.einsum('pviq,pkq->pvik', mixed.astype(jnp.float32), chosen.astype(jnp.float32))
        return result.astype(jnp.bfloat16)

    stacked = lax.map(one_sector, (jnp.moveaxis(vectors, 1, 0), left_env, sector_ids))
    stacked = jnp.transpose(stacked, (2, 0, 3, 1, 4))
    return stacked.reshape(VECS, SECTORS, BS, PAIRS * BS)
```

```python
import functools

import jax
import jax.numpy as jnp
from jax import lax
from jax.experimental import pallas as pl
from jax.experimental.pallas import tpu as pltpu
from jax.sharding import PartitionSpec as P


def phases_of(peers):
    bits = []
    bit = peers // 2
    while bit > 1:
        bits.append(bit)
        bit //= 2
    groups = [bits[:1]] if bits else []
    rest = bits[1:]
    while rest:
        groups.append(rest[:2])
        rest = rest[2:]
    if peers > 1:
        groups.append([1])
    return groups


def combos(group):
    sums = [0]
    for bit in group:
        sums = sums + [s ^ bit for s in sums]
    return sums[1:]


def place_of(apart, peers):
    place = jnp.zeros_like(apart)
    at = 0
    for group in phases_of(peers):
        for bit in group:
            place = place + (((apart // bit) % 2) << at)
            at += 1
    return place


def hop(x, apart, peers):
    return lax.ppermute(x, "sec", [(i, i ^ apart) for i in range(peers)])


def mix_kernel(left_ref, vec_ref, mixed_ref):
    vecs, secs, width, _ = vec_ref.shape
    terms = left_ref.shape[2] // width
    for a in range(secs):
        turned = left_ref[a].T
        for v in range(vecs):
            both = jnp.dot(turned, vec_ref[v, a], preferred_element_type=jnp.float32).astype(jnp.bfloat16)
            for w in range(terms):
                mixed_ref[a, w, v * width : (v + 1) * width, :] = both[w * width : (w + 1) * width]


def close_kernel(at_ref, mixed_ref, env_ref, out_ref, done_ref, sems):
    secs, terms, tall, wide = mixed_ref.shape
    width = env_ref.shape[1]
    pairs = wide // width
    vecs = tall // width
    lane = lax.broadcasted_iota(jnp.int32, (width, 2 * width), 1)
    low = lane < width
    copies = []
    for a in range(secs):
        for p in range(0, pairs, 2):
            first = env_ref[at_ref[a, p]]
            second = env_ref[at_ref[a, p + 1]]
            zero = jnp.zeros_like(first)
            top = [jnp.where(low, first, zero), jnp.where(low, pltpu.roll(first, width, 1), zero)]
            bottom = [jnp.where(low, zero, pltpu.roll(second, width, 1)), jnp.where(low, zero, second)]
            weights = jnp.concatenate([jnp.concatenate(top, 1), jnp.concatenate(bottom, 1)], 0)
            cols = slice(p * width, (p + 2) * width)
            rows = jnp.concatenate([mixed_ref[a, w, :, cols] for w in range(terms)], 1)
            block = lax.dot_general(
                rows, weights, (((1,), (1,)), ((), ())), preferred_element_type=jnp.float32
            ).astype(jnp.bfloat16)
            for v in range(vecs):
                done_ref[v, a, :, cols] = block[v * width : (v + 1) * width]
        copy = pltpu.make_async_copy(done_ref.at[:, a], out_ref.at[:, a], sems.at[a])
        copy.start()
        copies.append(copy)
    for copy in copies:
        copy.wait()


def body(vectors, left_env, right_env, target_device, target_slot):
    peers = lax.axis_size("sec")
    vecs, secs, width, wide = vectors.shape
    pairs = wide // width
    terms = left_env.shape[2] // width
    me = lax.axis_index("sec")
    dest = target_device.reshape(secs, pairs)
    at = place_of(dest ^ me, peers) * secs + target_slot
    mixed = pl.pallas_call(
        mix_kernel,
        out_shape=jax.ShapeDtypeStruct((secs, terms, vecs * width, wide), jnp.bfloat16),
        cost_estimate=pl.CostEstimate(
            flops=2 * vecs * secs * terms * width * width * wide,
            bytes_accessed=6 * vecs * secs * width * wide,
            transcendentals=0,
        ),
    )(left_env, vectors)
    env = right_env
    for group in phases_of(peers):
        env = jnp.concatenate([env] + [hop(env, s, peers) for s in combos(group)], 0)
    return pl.pallas_call(
        close_kernel,
        out_shape=jax.ShapeDtypeStruct(vectors.shape, jnp.bfloat16),
        in_specs=[
            pl.BlockSpec(memory_space=pltpu.SMEM),
            pl.BlockSpec(memory_space=pltpu.VMEM),
            pl.BlockSpec(memory_space=pltpu.VMEM),
        ],
        out_specs=pl.BlockSpec(memory_space=pl.ANY),
        scratch_shapes=[pltpu.VMEM(vectors.shape, jnp.bfloat16), pltpu.SemaphoreType.DMA((secs,))],
        cost_estimate=pl.CostEstimate(
            flops=2 * vecs * secs * terms * width * width * wide,
            bytes_accessed=6 * vecs * secs * width * wide,
            transcendentals=0,
        ),
    )(at, mixed, env)


def solution(mesh):
    return jax.shard_map(
        body,
        mesh=mesh,
        in_specs=(
            P(None, ("grp", "sec"), None, None),
            P(("grp", "sec"), None, None),
            P(("grp", "sec"), None, None),
            P(("grp", "sec"), None, None),
            P(("grp", "sec"), None),
        ),
        out_specs=P(None, ("grp", "sec"), None, None),
        check_vma=False,
    )
```

```python
import functools

import jax
import jax.numpy as jnp
from jax import lax
from jax.experimental import pallas as pl
from jax.experimental.pallas import tpu as pltpu
from jax.sharding import PartitionSpec as P


def phases_of(peers):
    bits = []
    bit = peers // 2
    while bit > 1:
        bits.append(bit)
        bit //= 2
    groups = [bits[:1]] if bits else []
    rest = bits[1:]
    while rest:
        groups.append(rest[:2])
        rest = rest[2:]
    if peers > 1:
        groups.append([1])
    return groups


def combos(group):
    sums = [0]
    for bit in group:
        sums = sums + [s ^ bit for s in sums]
    return sums[1:]


def place_of(apart, peers):
    place = 0
    at = 0
    for group in phases_of(peers):
        for bit in group:
            place = place + (((apart // bit) & 1) << at)
            at += 1
    return place


def hop(x, apart, peers):
    return lax.ppermute(x, "sec", [(i, i ^ apart) for i in range(peers)])


def mix_kernel(left_hbm, vec_hbm, env_hbm, mixed_ref, own_ref, left_ref, vec_ref, sems):
    copies = [
        pltpu.make_async_copy(left_hbm, left_ref, sems.at[0]),
        pltpu.make_async_copy(vec_hbm.at[:, 0], vec_ref.at[:, 0], sems.at[1]),
        pltpu.make_async_copy(vec_hbm.at[:, 1], vec_ref.at[:, 1], sems.at[2]),
        pltpu.make_async_copy(env_hbm, own_ref, sems.at[3]),
    ]
    for copy in copies:
        copy.start()
    for copy in copies:
        copy.wait()
    vecs, secs, width, _ = vec_ref.shape
    terms = left_ref.shape[2] // width
    for a in range(secs):
        turned = left_ref[a].T
        for v in range(vecs):
            both = jnp.dot(turned, vec_ref[v, a], preferred_element_type=jnp.float32).astype(jnp.bfloat16)
            for w in range(terms):
                mixed_ref[a, w, v * width : (v + 1) * width, :] = both[w * width : (w + 1) * width]


def close_kernel(peers, dest_ref, slot_ref, mixed_ref, env_ref, out_ref, done_ref, sems):
    secs, terms, tall, wide = mixed_ref.shape
    width = env_ref.shape[1]
    pairs = wide // width
    vecs = tall // width
    lane = lax.broadcasted_iota(jnp.int32, (width, 2 * width), 1)
    low = lane < width
    copies = []
    me = lax.axis_index("sec")

    def env_at(a, p):
        return env_ref[place_of(dest_ref[a, p] ^ me, peers) * secs + slot_ref[a, p]]

    for a in range(secs):
        for p in range(0, pairs, 2):
            first = env_at(a, p)
            second = env_at(a, p + 1)
            zero = jnp.zeros_like(first)
            top = [jnp.where(low, first, zero), jnp.where(low, pltpu.roll(first, width, 1), zero)]
            bottom = [jnp.where(low, zero, pltpu.roll(second, width, 1)), jnp.where(low, zero, second)]
            weights = jnp.concatenate([jnp.concatenate(top, 1), jnp.concatenate(bottom, 1)], 0)
            cols = slice(p * width, (p + 2) * width)
            rows = jnp.concatenate([mixed_ref[a, w, :, cols] for w in range(terms)], 1)
            block = lax.dot_general(
                rows, weights, (((1,), (1,)), ((), ())), preferred_element_type=jnp.float32
            ).astype(jnp.bfloat16)
            for v in range(vecs):
                done_ref[v, a, :, cols] = block[v * width : (v + 1) * width]
        copy = pltpu.make_async_copy(done_ref.at[:, a], out_ref.at[:, a], sems.at[a])
        copy.start()
        copies.append(copy)
    for copy in copies:
        copy.wait()


def body(vectors, left_env, right_env, target_device, target_slot):
    peers = lax.axis_size("sec")
    vecs, secs, width, wide = vectors.shape
    pairs = wide // width
    terms = left_env.shape[2] // width
    dest = target_device.reshape(secs, pairs)
    mixed, own = pl.pallas_call(
        mix_kernel,
        out_shape=(
            jax.ShapeDtypeStruct((secs, terms, vecs * width, wide), jnp.bfloat16),
            jax.ShapeDtypeStruct(right_env.shape, right_env.dtype),
        ),
        in_specs=[pl.BlockSpec(memory_space=pltpu.HBM)] * 3,
        scratch_shapes=[
            pltpu.VMEM(left_env.shape, jnp.bfloat16),
            pltpu.VMEM(vectors.shape, jnp.bfloat16),
            pltpu.SemaphoreType.DMA((4,)),
        ],
        compiler_params=pltpu.CompilerParams(vmem_limit_bytes=16 * 2**20),
        cost_estimate=pl.CostEstimate(
            flops=2 * vecs * secs * terms * width * width * wide,
            bytes_accessed=6 * vecs * secs * width * wide,
            transcendentals=0,
        ),
    )(*[pltpu.with_memory_space_constraint(x, pltpu.HBM) for x in (left_env, vectors, right_env)])
    env, kept = right_env, own
    for group in phases_of(peers):
        env = kept = jnp.concatenate([kept] + [hop(env, s, peers) for s in combos(group)], 0)
    return pl.pallas_call(
        functools.partial(close_kernel, peers),
        out_shape=jax.ShapeDtypeStruct(vectors.shape, jnp.bfloat16),
        in_specs=[
            pl.BlockSpec(memory_space=pltpu.SMEM),
            pl.BlockSpec(memory_space=pltpu.SMEM),
            pl.BlockSpec(memory_space=pltpu.VMEM),
            pl.BlockSpec(memory_space=pltpu.VMEM),
        ],
        out_specs=pl.BlockSpec(memory_space=pl.ANY),
        scratch_shapes=[pltpu.VMEM(vectors.shape, jnp.bfloat16), pltpu.SemaphoreType.DMA((secs,))],
        compiler_params=pltpu.CompilerParams(vmem_limit_bytes=16 * 2**20),
        cost_estimate=pl.CostEstimate(
            flops=2 * vecs * secs * terms * width * width * wide,
            bytes_accessed=6 * vecs * secs * width * wide,
            transcendentals=0,
        ),
    )(dest, target_slot, mixed, env)


def solution(mesh):
    return jax.shard_map(
        body,
        mesh=mesh,
        in_specs=(
            P(None, ("grp", "sec"), None, None),
            P(("grp", "sec"), None, None),
            P(("grp", "sec"), None, None),
            P(("grp", "sec"), None, None),
            P(("grp", "sec"), None),
        ),
        out_specs=P(None, ("grp", "sec"), None, None),
        check_vma=False,
    )
```

```python
import functools

import jax
import jax.numpy as jnp
from jax import lax
from jax.experimental import pallas as pl
from jax.experimental.pallas import tpu as pltpu
from jax.sharding import PartitionSpec as P


def phases_of(peers):
    bits = []
    bit = peers // 2
    while bit > 1:
        bits.append(bit)
        bit //= 2
    groups = [[(bits[0], bits[0])]] if bits else []
    for i in range(1, len(bits), 2):
        if i + 1 == len(bits):
            groups.append([(bits[i], bits[i])])
        else:
            high, low = bits[i], bits[i + 1]
            groups.append([(high | low, high), (low, high | low)])
    return groups


def combos(group):
    sums = [0]
    for mask, _ in group:
        sums = sums + [s ^ mask for s in sums]
    return sums[1:]


def parity(x, test):
    total, bit = 0, 1
    while bit <= test:
        if test & bit:
            total = total ^ ((x // bit) & 1)
        bit *= 2
    return total


def place_of(apart, peers):
    place = 0
    at = 0
    flips = apart & 1
    for group in phases_of(peers):
        some = 0
        for mask, test in group:
            own = parity(apart, test)
            place = place + (own << at)
            some = some | own
            at += 1
        flips = flips ^ some
    return place + (flips << at)


def hop(x, apart, peers):
    return lax.ppermute(x, "sec", [(i, i ^ apart) for i in range(peers)])


def mix_kernel(left_hbm, vec_hbm, env_hbm, mixed_ref, own_ref, left_ref, vec_ref, sems):
    copies = [
        pltpu.make_async_copy(left_hbm, left_ref, sems.at[0]),
        pltpu.make_async_copy(vec_hbm.at[:, 0], vec_ref.at[:, 0], sems.at[1]),
        pltpu.make_async_copy(vec_hbm.at[:, 1], vec_ref.at[:, 1], sems.at[2]),
        pltpu.make_async_copy(env_hbm, own_ref, sems.at[3]),
    ]
    for copy in copies:
        copy.start()
    for copy in copies:
        copy.wait()
    vecs, secs, width, _ = vec_ref.shape
    terms = left_ref.shape[2] // width
    for a in range(secs):
        turned = left_ref[a].T
        for v in range(vecs):
            both = jnp.dot(turned, vec_ref[v, a], preferred_element_type=jnp.float32).astype(jnp.bfloat16)
            for w in range(terms):
                mixed_ref[a, w, v * width : (v + 1) * width, :] = both[w * width : (w + 1) * width]


def close_kernel(peers, dest_ref, slot_ref, mixed_ref, env_ref, out_ref, done_ref, sems):
    secs, terms, tall, wide = mixed_ref.shape
    width = env_ref.shape[1]
    pairs = wide // width
    vecs = tall // width
    lane = lax.broadcasted_iota(jnp.int32, (width, 2 * width), 1)
    low = lane < width
    copies = []
    me = lax.axis_index("sec")

    def env_at(a, p):
        return env_ref[place_of(dest_ref[a, p] ^ me, peers) * secs + slot_ref[a, p]]

    for a in range(secs):
        for p in range(0, pairs, 2):
            first = env_at(a, p)
            second = env_at(a, p + 1)
            zero = jnp.zeros_like(first)
            top = [jnp.where(low, first, zero), jnp.where(low, pltpu.roll(first, width, 1), zero)]
            bottom = [jnp.where(low, zero, pltpu.roll(second, width, 1)), jnp.where(low, zero, second)]
            weights = jnp.concatenate([jnp.concatenate(top, 1), jnp.concatenate(bottom, 1)], 0)
            cols = slice(p * width, (p + 2) * width)
            rows = jnp.concatenate([mixed_ref[a, w, :, cols] for w in range(terms)], 1)
            block = lax.dot_general(
                rows, weights, (((1,), (1,)), ((), ())), preferred_element_type=jnp.float32
            ).astype(jnp.bfloat16)
            for v in range(vecs):
                done_ref[v, a, :, cols] = block[v * width : (v + 1) * width]
        copy = pltpu.make_async_copy(done_ref.at[:, a], out_ref.at[:, a], sems.at[a])
        copy.start()
        copies.append(copy)
    for copy in copies:
        copy.wait()


def body(vectors, left_env, right_env, target_device, target_slot):
    peers = lax.axis_size("sec")
    vecs, secs, width, wide = vectors.shape
    pairs = wide // width
    terms = left_env.shape[2] // width
    dest = target_device.reshape(secs, pairs)
    mixed, own = pl.pallas_call(
        mix_kernel,
        out_shape=(
            jax.ShapeDtypeStruct((secs, terms, vecs * width, wide), jnp.bfloat16),
            jax.ShapeDtypeStruct(right_env.shape, right_env.dtype),
        ),
        in_specs=[pl.BlockSpec(memory_space=pltpu.HBM)] * 3,
        scratch_shapes=[
            pltpu.VMEM(left_env.shape, jnp.bfloat16),
            pltpu.VMEM(vectors.shape, jnp.bfloat16),
            pltpu.SemaphoreType.DMA((4,)),
        ],
        compiler_params=pltpu.CompilerParams(vmem_limit_bytes=16 * 2**20),
        cost_estimate=pl.CostEstimate(
            flops=2 * vecs * secs * terms * width * width * wide,
            bytes_accessed=6 * vecs * secs * width * wide,
            transcendentals=0,
        ),
    )(*[pltpu.with_memory_space_constraint(x, pltpu.HBM) for x in (left_env, vectors, right_env)])
    env, kept = right_env, own
    for group in phases_of(peers):
        env = kept = jnp.concatenate([kept] + [hop(env, s | 1, peers) for s in combos(group)], 0)
    if peers > 1:
        env = jnp.concatenate([env, hop(env, 1, peers)], 0)
    return pl.pallas_call(
        functools.partial(close_kernel, peers),
        out_shape=jax.ShapeDtypeStruct(vectors.shape, jnp.bfloat16),
        in_specs=[
            pl.BlockSpec(memory_space=pltpu.SMEM),
            pl.BlockSpec(memory_space=pltpu.SMEM),
            pl.BlockSpec(memory_space=pltpu.VMEM),
            pl.BlockSpec(memory_space=pltpu.VMEM),
        ],
        out_specs=pl.BlockSpec(memory_space=pl.ANY),
        scratch_shapes=[pltpu.VMEM(vectors.shape, jnp.bfloat16), pltpu.SemaphoreType.DMA((secs,))],
        compiler_params=pltpu.CompilerParams(vmem_limit_bytes=16 * 2**20),
        cost_estimate=pl.CostEstimate(
            flops=2 * vecs * secs * terms * width * width * wide,
            bytes_accessed=6 * vecs * secs * width * wide,
            transcendentals=0,
        ),
    )(dest, target_slot, mixed, env)


def solution(mesh):
    return jax.shard_map(
        body,
        mesh=mesh,
        in_specs=(
            P(None, ("grp", "sec"), None, None),
            P(("grp", "sec"), None, None),
            P(("grp", "sec"), None, None),
            P(("grp", "sec"), None, None),
            P(("grp", "sec"), None),
        ),
        out_specs=P(None, ("grp", "sec"), None, None),
        check_vma=False,
    )
```

```python
import functools

import jax
import jax.numpy as jnp
from jax import lax
from jax.experimental import pallas as pl
from jax.experimental.pallas import tpu as pltpu
from jax.sharding import PartitionSpec as P


def phases_of(peers):
    bits = []
    bit = peers // 2
    while bit > 1:
        bits.append(bit)
        bit //= 2
    groups = [[(bits[0], bits[0])]] if bits else []
    for i in range(1, len(bits), 2):
        if i + 1 == len(bits):
            groups.append([(bits[i], bits[i])])
        else:
            high, low = bits[i], bits[i + 1]
            groups.append([(high | low, high), (low, high | low)])
    return groups


def combos(group):
    sums = [0]
    for mask, _ in group:
        sums = sums + [s ^ mask for s in sums]
    return sums[1:]


def parity(x, test):
    total, bit = 0, 1
    while bit <= test:
        if test & bit:
            total = total ^ ((x // bit) & 1)
        bit *= 2
    return total


def place_of(apart, peers):
    place = 0
    at = 0
    flips = apart & 1
    for group in phases_of(peers):
        some = 0
        for mask, test in group:
            own = parity(apart, test)
            place = place + (own << at)
            some = some | own
            at += 1
        flips = flips ^ some
    return place + (flips << at)


def hop(x, apart, peers):
    return lax.ppermute(x, "sec", [(i, i ^ apart) for i in range(peers)])


def mix_kernel(peers, left_hbm, vec_hbm, env_hbm, dest_hbm, slot_hbm, mixed_ref, own_ref, at_ref, left_ref, vec_ref, dest_ref, slot_ref, sems):
    copies = [
        pltpu.make_async_copy(left_hbm, left_ref, sems.at[0]),
        pltpu.make_async_copy(vec_hbm.at[:, 0], vec_ref.at[:, 0], sems.at[1]),
        pltpu.make_async_copy(vec_hbm.at[:, 1], vec_ref.at[:, 1], sems.at[2]),
        pltpu.make_async_copy(env_hbm, own_ref, sems.at[3]),
        pltpu.make_async_copy(dest_hbm, dest_ref, sems.at[4]),
        pltpu.make_async_copy(slot_hbm, slot_ref, sems.at[5]),
    ]
    for copy in copies:
        copy.start()
    for copy in copies:
        copy.wait()
    me = lax.axis_index("sec")
    at_ref[...] = place_of(dest_ref[...] ^ me, peers) * vec_ref.shape[1] + slot_ref[...]
    vecs, secs, width, wide = vec_ref.shape
    low = lax.broadcasted_iota(jnp.int32, (width, wide), 1) % (2 * width) < width

    def turn(x):
        parts = [
            pltpu.roll(x[:, c : c + 2 * width], width, 1) for c in range(0, wide, 2 * width)
        ]
        return jnp.concatenate(parts, 1)

    for a in range(secs):
        turned = left_ref[a].T
        for v in range(vecs):
            both = jnp.dot(turned, vec_ref[v, a], preferred_element_type=jnp.float32).astype(jnp.bfloat16)
            first, second = both[:width], both[width:]
            mixed_ref[a, 0, v * width : (v + 1) * width, :] = jnp.where(low, first, turn(second))
            mixed_ref[a, 1, v * width : (v + 1) * width, :] = jnp.where(low, turn(first), second)


def close_kernel(at_ref, mixed_ref, env_ref, out_ref, done_ref, sems):
    secs, terms, tall, wide = mixed_ref.shape
    width = env_ref.shape[1]
    pairs = wide // width
    vecs = tall // width
    copies = []

    where = at_ref[...]

    def env_at(a, p):
        return env_ref[where[a, p]]

    for a in range(secs):
        for p in range(0, pairs, 2):
            first = env_at(a, p)
            second = env_at(a, p + 1)
            zero = jnp.zeros_like(first)
            top = jnp.concatenate([first, zero], 1)
            bottom = jnp.concatenate([zero, second], 1)
            weights = jnp.concatenate([top, bottom], 0)
            cols = slice(p * width, (p + 2) * width)
            rows = jnp.concatenate([mixed_ref[a, w, :, cols] for w in range(2)], 1)
            block = lax.dot_general(
                rows, weights, (((1,), (1,)), ((), ())), preferred_element_type=jnp.float32
            ).astype(jnp.bfloat16)
            for v in range(vecs):
                done_ref[v, a, :, cols] = block[v * width : (v + 1) * width]
        copy = pltpu.make_async_copy(done_ref.at[:, a], out_ref.at[:, a], sems.at[a])
        copy.start()
        copies.append(copy)
    for copy in copies:
        copy.wait()


def body(vectors, left_env, right_env, target_device, target_slot):
    peers = lax.axis_size("sec")
    vecs, secs, width, wide = vectors.shape
    pairs = wide // width
    terms = left_env.shape[2] // width
    dest = target_device.reshape(secs, pairs)
    mixed, own, at = pl.pallas_call(
        functools.partial(mix_kernel, peers),
        out_shape=(
            jax.ShapeDtypeStruct((secs, terms, vecs * width, wide), jnp.bfloat16),
            jax.ShapeDtypeStruct(right_env.shape, right_env.dtype),
            jax.ShapeDtypeStruct(target_slot.shape, jnp.int32),
        ),
        in_specs=[pl.BlockSpec(memory_space=pltpu.HBM)] * 5,
        scratch_shapes=[
            pltpu.VMEM(left_env.shape, jnp.bfloat16),
            pltpu.VMEM(vectors.shape, jnp.bfloat16),
            pltpu.VMEM(dest.shape, jnp.int32),
            pltpu.VMEM(target_slot.shape, jnp.int32),
            pltpu.SemaphoreType.DMA((6,)),
        ],
        compiler_params=pltpu.CompilerParams(vmem_limit_bytes=16 * 2**20),
        cost_estimate=pl.CostEstimate(
            flops=2 * vecs * secs * terms * width * width * wide,
            bytes_accessed=6 * vecs * secs * width * wide,
            transcendentals=0,
        ),
    )(*[pltpu.with_memory_space_constraint(x, pltpu.HBM) for x in (left_env, vectors, right_env, dest, target_slot)])
    env, kept = right_env, own
    for group in phases_of(peers):
        env = kept = jnp.concatenate([kept] + [hop(env, s | 1, peers) for s in combos(group)], 0)
    if peers > 1:
        env = jnp.concatenate([env, hop(env, 1, peers)], 0)
    return pl.pallas_call(
        close_kernel,
        out_shape=jax.ShapeDtypeStruct(vectors.shape, jnp.bfloat16),
        in_specs=[
            pl.BlockSpec(memory_space=pltpu.VMEM),
            pl.BlockSpec(memory_space=pltpu.VMEM),
            pl.BlockSpec(memory_space=pltpu.VMEM),
        ],
        out_specs=pl.BlockSpec(memory_space=pl.ANY),
        scratch_shapes=[pltpu.VMEM(vectors.shape, jnp.bfloat16), pltpu.SemaphoreType.DMA((secs,))],
        compiler_params=pltpu.CompilerParams(vmem_limit_bytes=16 * 2**20),
        cost_estimate=pl.CostEstimate(
            flops=2 * vecs * secs * terms * width * width * wide,
            bytes_accessed=6 * vecs * secs * width * wide,
            transcendentals=0,
        ),
    )(at, mixed, env)


def solution(mesh):
    return jax.shard_map(
        body,
        mesh=mesh,
        in_specs=(
            P(None, ("grp", "sec"), None, None),
            P(("grp", "sec"), None, None),
            P(("grp", "sec"), None, None),
            P(("grp", "sec"), None, None),
            P(("grp", "sec"), None),
        ),
        out_specs=P(None, ("grp", "sec"), None, None),
        check_vma=False,
    )
```

```python
import functools

import jax
import jax.numpy as jnp
from jax import lax
from jax.experimental import pallas as pl
from jax.experimental.pallas import tpu as pltpu
from jax.sharding import PartitionSpec as P


def phases_of(peers):
    bits = []
    bit = peers // 2
    while bit > 1:
        bits.append(bit)
        bit //= 2
    groups = [[(bits[0], bits[0])]] if bits else []
    for i in range(1, len(bits), 2):
        if i + 1 == len(bits):
            groups.append([(bits[i], bits[i])])
        else:
            high, low = bits[i], bits[i + 1]
            groups.append([(high, high | low), (high | low, low)])
    return groups


def combos(group):
    sums = [0]
    for mask, _ in group:
        sums = sums + [s ^ mask for s in sums]
    return sums[1:]


def parity(x, test):
    total, bit = 0, 1
    while bit <= test:
        if test & bit:
            total = total ^ ((x // bit) & 1)
        bit *= 2
    return total


def place_of(apart, peers):
    place = 0
    at = 0
    flips = apart & 1
    for turn, group in enumerate(phases_of(peers)):
        some = 0
        for mask, test in group:
            own = parity(apart, test)
            place = place + (own << at)
            some = some | own
            at += 1
        if turn > 0:
            place = place ^ (1 << (at - 1))
        flips = flips ^ some
    return place + (flips << at)


def hop(x, apart, peers):
    return lax.ppermute(x, "sec", [(i, i ^ apart) for i in range(peers)])


def mix_kernel(peers, left_hbm, vec_hbm, dest_hbm, slot_hbm, env_ref, mixed_ref, kept_ref, at_ref, left_ref, vec_ref, dest_ref, slot_ref, sems):
    copies = [
        pltpu.make_async_copy(left_hbm, left_ref, sems.at[0]),
        pltpu.make_async_copy(vec_hbm.at[:, 0], vec_ref.at[:, 0], sems.at[1]),
        pltpu.make_async_copy(vec_hbm.at[:, 1], vec_ref.at[:, 1], sems.at[2]),
        pltpu.make_async_copy(dest_hbm, dest_ref, sems.at[3]),
        pltpu.make_async_copy(slot_hbm, slot_ref, sems.at[4]),
    ]
    for copy in copies:
        copy.start()
    kept_ref[...] = env_ref[...]
    for copy in copies:
        copy.wait()
    me = lax.axis_index("sec")
    at_ref[...] = place_of(dest_ref[...] ^ me, peers) * vec_ref.shape[1] + slot_ref[...]
    vecs, secs, width, wide = vec_ref.shape
    low = lax.broadcasted_iota(jnp.int32, (width, wide), 1) % (2 * width) < width

    def turn(x):
        parts = [
            pltpu.roll(x[:, c : c + 2 * width], width, 1) for c in range(0, wide, 2 * width)
        ]
        return jnp.concatenate(parts, 1)

    for a in range(secs):
        turned = left_ref[a].T
        for v in range(vecs):
            both = jnp.dot(turned, vec_ref[v, a], preferred_element_type=jnp.float32).astype(jnp.bfloat16)
            first, second = both[:width], both[width:]
            mixed_ref[a, 0, v * width : (v + 1) * width, :] = jnp.where(low, first, turn(second))
            mixed_ref[a, 1, v * width : (v + 1) * width, :] = jnp.where(low, turn(first), second)


def close_kernel(at_ref, mixed_ref, env_ref, out_ref, done_ref, sems):
    secs, terms, tall, wide = mixed_ref.shape
    width = env_ref.shape[1]
    pairs = wide // width
    vecs = tall // width
    copies = []

    where = at_ref[...]

    def env_at(a, p):
        return env_ref[where[a, p]]

    for a in range(secs):
        for p in range(0, pairs, 2):
            first = env_at(a, p)
            second = env_at(a, p + 1)
            zero = jnp.zeros_like(first)
            top = jnp.concatenate([first, zero], 1)
            bottom = jnp.concatenate([zero, second], 1)
            weights = jnp.concatenate([top, bottom], 0)
            cols = slice(p * width, (p + 2) * width)
            rows = jnp.concatenate([mixed_ref[a, w, :, cols] for w in range(2)], 1)
            block = lax.dot_general(
                rows, weights, (((1,), (1,)), ((), ())), preferred_element_type=jnp.float32
            ).astype(jnp.bfloat16)
            for v in range(vecs):
                done_ref[v, a, :, cols] = block[v * width : (v + 1) * width]
        copy = pltpu.make_async_copy(done_ref.at[:, a], out_ref.at[:, a], sems.at[a])
        copy.start()
        copies.append(copy)
    for copy in copies:
        copy.wait()


def body(vectors, left_env, right_env, target_device, target_slot):
    peers = lax.axis_size("sec")
    vecs, secs, width, wide = vectors.shape
    pairs = wide // width
    terms = left_env.shape[2] // width
    dest = target_device.reshape(secs, pairs)
    groups = phases_of(peers)
    env = right_env
    for group in groups[:1]:
        env = jnp.concatenate([env] + [hop(env, s | 1, peers) for s in combos(group)], 0)
    mixed, kept, at = pl.pallas_call(
        functools.partial(mix_kernel, peers),
        out_shape=(
            jax.ShapeDtypeStruct((secs, terms, vecs * width, wide), jnp.bfloat16),
            jax.ShapeDtypeStruct(env.shape, env.dtype),
            jax.ShapeDtypeStruct(target_slot.shape, jnp.int32),
        ),
        in_specs=[pl.BlockSpec(memory_space=pltpu.HBM)] * 4 + [pl.BlockSpec(memory_space=pltpu.VMEM)],
        scratch_shapes=[
            pltpu.VMEM(left_env.shape, jnp.bfloat16),
            pltpu.VMEM(vectors.shape, jnp.bfloat16),
            pltpu.VMEM(dest.shape, jnp.int32),
            pltpu.VMEM(target_slot.shape, jnp.int32),
            pltpu.SemaphoreType.DMA((5,)),
        ],
        compiler_params=pltpu.CompilerParams(vmem_limit_bytes=16 * 2**20),
        cost_estimate=pl.CostEstimate(
            flops=2 * vecs * secs * terms * width * width * wide,
            bytes_accessed=6 * vecs * secs * width * wide,
            transcendentals=0,
        ),
    )(*[pltpu.with_memory_space_constraint(x, pltpu.HBM) for x in (left_env, vectors, dest, target_slot)], env)
    for group in groups[1:]:
        pieces = [kept] + [hop(env, s | 1, peers) for s in combos(group)]
        half = len(pieces) // 2
        pieces = pieces[half:] + pieces[:half]
        env = kept = jnp.concatenate(pieces, 0)
    if peers > 1:
        half = env.shape[0] // 2
        env = jnp.concatenate([env, hop(env[:half], 1, peers), hop(env[half:], 1, peers)], 0)
    return pl.pallas_call(
        close_kernel,
        out_shape=jax.ShapeDtypeStruct(vectors.shape, jnp.bfloat16),
        in_specs=[
            pl.BlockSpec(memory_space=pltpu.VMEM),
            pl.BlockSpec(memory_space=pltpu.VMEM),
            pl.BlockSpec(memory_space=pltpu.VMEM),
        ],
        out_specs=pl.BlockSpec(memory_space=pl.ANY),
        scratch_shapes=[pltpu.VMEM(vectors.shape, jnp.bfloat16), pltpu.SemaphoreType.DMA((secs,))],
        compiler_params=pltpu.CompilerParams(vmem_limit_bytes=16 * 2**20),
        cost_estimate=pl.CostEstimate(
            flops=2 * vecs * secs * terms * width * width * wide,
            bytes_accessed=6 * vecs * secs * width * wide,
            transcendentals=0,
        ),
    )(at, mixed, env)


def solution(mesh):
    return jax.shard_map(
        body,
        mesh=mesh,
        in_specs=(
            P(None, ("grp", "sec"), None, None),
            P(("grp", "sec"), None, None),
            P(("grp", "sec"), None, None),
            P(("grp", "sec"), None, None),
            P(("grp", "sec"), None),
        ),
        out_specs=P(None, ("grp", "sec"), None, None),
        check_vma=False,
    )
```

```python
import functools

import jax
import jax.numpy as jnp
from jax import lax
from jax.experimental import pallas as pl
from jax.experimental.pallas import tpu as pltpu
from jax.sharding import PartitionSpec as P


def bits_of(peers):
    bits = []
    bit = peers // 2
    while bit > 1:
        bits.append(bit)
        bit //= 2
    return bits


def shift(blocks, step):
    return [x ^ step for x in blocks]


def layout_of(peers):
    bits = bits_of(peers)
    blocks = [0] + [bit | 1 for bit in bits[:1]]
    if len(bits) == 3:
        first, high, low = [bit | 1 for bit in bits]
        both = (bits[1] ^ bits[2]) | 1
        early = [low] + shift([0, first], both) + blocks
        late = [low ^ first] + shift([0, first], high)
        blocks = early + late
    else:
        for bit in bits[1:]:
            blocks = blocks + shift(blocks, bit | 1)
    if peers > 1:
        blocks = blocks + shift(blocks, 1)
    return blocks


def place_of(apart, peers):
    place = jnp.zeros_like(apart)
    for at, x in enumerate(layout_of(peers)):
        place = jnp.where(apart == x, at, place)
    return place


def hop(x, apart, peers):
    return lax.ppermute(x, "sec", [(i, i ^ apart) for i in range(peers)])


def mix_kernel(peers, left_hbm, vec_hbm, dest_hbm, slot_hbm, env_ref, mixed_ref, kept_ref, at_ref, left_ref, vec_ref, dest_ref, slot_ref, sems):
    copies = [
        pltpu.make_async_copy(left_hbm, left_ref, sems.at[0]),
        pltpu.make_async_copy(vec_hbm, vec_ref, sems.at[1]),
        pltpu.make_async_copy(dest_hbm, dest_ref, sems.at[2]),
        pltpu.make_async_copy(slot_hbm, slot_ref, sems.at[3]),
    ]
    for copy in copies:
        copy.start()
    kept_ref[...] = env_ref[...]
    for copy in copies:
        copy.wait()
    me = lax.axis_index("sec")
    at_ref[...] = place_of(dest_ref[...] ^ me, peers) * vec_ref.shape[1] + slot_ref[...]
    vecs, secs, width, wide = vec_ref.shape
    low = lax.broadcasted_iota(jnp.int32, (width, wide), 1) % (2 * width) < width

    def turn(x):
        parts = [
            pltpu.roll(x[:, c : c + 2 * width], width, 1) for c in range(0, wide, 2 * width)
        ]
        return jnp.concatenate(parts, 1)

    for a in range(secs):
        turned = left_ref[a].T
        for v in range(vecs):
            both = jnp.dot(turned, vec_ref[v, a], preferred_element_type=jnp.float32).astype(jnp.bfloat16)
            first, second = both[:width], both[width:]
            mixed_ref[a, 0, v * width : (v + 1) * width, :] = jnp.where(low, first, turn(second))
            mixed_ref[a, 1, v * width : (v + 1) * width, :] = jnp.where(low, turn(first), second)


def close_kernel(at_ref, mixed_ref, env_ref, out_ref, done_ref, sems):
    secs, terms, tall, wide = mixed_ref.shape
    width = env_ref.shape[1]
    pairs = wide // width
    vecs = tall // width
    copies = []

    where = at_ref[...]

    def env_at(a, p):
        return env_ref[where[a, p]]

    for a in range(secs):
        for p in range(0, pairs, 2):
            first = env_at(a, p)
            second = env_at(a, p + 1)
            zero = jnp.zeros_like(first)
            top = jnp.concatenate([first, zero], 1)
            bottom = jnp.concatenate([zero, second], 1)
            weights = jnp.concatenate([top, bottom], 0)
            cols = slice(p * width, (p + 2) * width)
            rows = jnp.concatenate([mixed_ref[a, w, :, cols] for w in range(2)], 1)
            block = lax.dot_general(
                rows, weights, (((1,), (1,)), ((), ())), preferred_element_type=jnp.float32
            ).astype(jnp.bfloat16)
            for v in range(vecs):
                done_ref[v, a, :, cols] = block[v * width : (v + 1) * width]
        copy = pltpu.make_async_copy(done_ref.at[:, a], out_ref.at[:, a], sems.at[a])
        copy.start()
        copies.append(copy)
    for copy in copies:
        copy.wait()


def body(vectors, left_env, right_env, target_device, target_slot):
    peers = lax.axis_size("sec")
    vecs, secs, width, wide = vectors.shape
    pairs = wide // width
    terms = left_env.shape[2] // width
    dest = target_device.reshape(secs, pairs)
    bits = bits_of(peers)
    env = right_env
    paired = len(bits) == 3
    if bits:
        far = hop(right_env, bits[0] | 1, peers)
        if paired:
            near = hop(right_env, bits[2] | 1, peers)
        env = jnp.concatenate([right_env, far], 0)
    mixed, kept, at = pl.pallas_call(
        functools.partial(mix_kernel, peers),
        out_shape=(
            jax.ShapeDtypeStruct((secs, terms, vecs * width, wide), jnp.bfloat16),
            jax.ShapeDtypeStruct(env.shape, env.dtype),
            jax.ShapeDtypeStruct(target_slot.shape, jnp.int32),
        ),
        in_specs=[pl.BlockSpec(memory_space=pltpu.HBM)] * 4 + [pl.BlockSpec(memory_space=pltpu.VMEM)],
        scratch_shapes=[
            pltpu.VMEM(left_env.shape, jnp.bfloat16),
            pltpu.VMEM(vectors.shape, jnp.bfloat16),
            pltpu.VMEM(dest.shape, jnp.int32),
            pltpu.VMEM(target_slot.shape, jnp.int32),
            pltpu.SemaphoreType.DMA((4,)),
        ],
        compiler_params=pltpu.CompilerParams(vmem_limit_bytes=16 * 2**20),
        cost_estimate=pl.CostEstimate(
            flops=2 * vecs * secs * terms * width * width * wide,
            bytes_accessed=6 * vecs * secs * width * wide,
            transcendentals=0,
        ),
    )(*[pltpu.with_memory_space_constraint(x, pltpu.HBM) for x in (left_env, vectors, dest, target_slot)], env)
    if paired:
        corner = hop(env, (bits[1] ^ bits[2]) | 1, peers)
        side = hop(env, bits[1] | 1, peers)
        rest = hop(far, bits[2] | 1, peers)
        early = jnp.concatenate([near, corner, kept], 0)
        late = jnp.concatenate([rest, side], 0)
        env = jnp.concatenate([early, late, hop(early, 1, peers), hop(late, 1, peers)], 0)
    else:
        for bit in bits[1:]:
            env = kept = jnp.concatenate([kept, hop(env, bit | 1, peers)], 0)
        if peers > 1:
            env = jnp.concatenate([kept, hop(env, 1, peers)], 0)
    return pl.pallas_call(
        close_kernel,
        out_shape=jax.ShapeDtypeStruct(vectors.shape, jnp.bfloat16),
        in_specs=[
            pl.BlockSpec(memory_space=pltpu.VMEM),
            pl.BlockSpec(memory_space=pltpu.VMEM),
            pl.BlockSpec(memory_space=pltpu.VMEM),
        ],
        out_specs=pl.BlockSpec(memory_space=pl.ANY),
        scratch_shapes=[pltpu.VMEM(vectors.shape, jnp.bfloat16), pltpu.SemaphoreType.DMA((secs,))],
        compiler_params=pltpu.CompilerParams(vmem_limit_bytes=16 * 2**20),
        cost_estimate=pl.CostEstimate(
            flops=2 * vecs * secs * terms * width * width * wide,
            bytes_accessed=6 * vecs * secs * width * wide,
            transcendentals=0,
        ),
    )(at, mixed, env)


def solution(mesh):
    return jax.shard_map(
        body,
        mesh=mesh,
        in_specs=(
            P(None, ("grp", "sec"), None, None),
            P(("grp", "sec"), None, None),
            P(("grp", "sec"), None, None),
            P(("grp", "sec"), None, None),
            P(("grp", "sec"), None),
        ),
        out_specs=P(None, ("grp", "sec"), None, None),
        check_vma=False,
    )
```

```python
import functools

import jax
import jax.numpy as jnp
from jax import lax
from jax.experimental import pallas as pl
from jax.experimental.pallas import tpu as pltpu
from jax.sharding import PartitionSpec as P


def bits_of(peers):
    bits = []
    bit = peers // 2
    while bit > 1:
        bits.append(bit)
        bit //= 2
    return bits


def shift(blocks, step):
    return [x ^ step for x in blocks]


def layout_of(peers):
    bits = bits_of(peers)
    blocks = [0] + [bit | 1 for bit in bits[:1]]
    if len(bits) == 3:
        first, high, low = [bit | 1 for bit in bits]
        both = (bits[1] ^ bits[2]) | 1
        early = [low] + shift([0, first], both) + blocks
        late = [low ^ first] + shift([0, first], high)
        blocks = early + late
    else:
        for bit in bits[1:]:
            blocks = blocks + shift(blocks, bit | 1)
    if peers > 1:
        blocks = blocks + shift(blocks, 1)
    return blocks


def place_of(apart, peers):
    place = jnp.zeros_like(apart)
    for at, x in enumerate(layout_of(peers)):
        place = jnp.where(apart == x, at, place)
    return place


def hop(x, apart, peers):
    return lax.ppermute(x, "sec", [(i, i ^ apart) for i in range(peers)])


def mix_kernel(peers, left_hbm, vec_hbm, dest_hbm, slot_hbm, env_ref, mixed_ref, kept_ref, at_ref, left_ref, vec_ref, dest_ref, slot_ref, sems):
    copies = [
        pltpu.make_async_copy(left_hbm, left_ref, sems.at[0]),
        pltpu.make_async_copy(vec_hbm, vec_ref, sems.at[1]),
        pltpu.make_async_copy(dest_hbm, dest_ref, sems.at[2]),
        pltpu.make_async_copy(slot_hbm, slot_ref, sems.at[3]),
    ]
    for copy in copies:
        copy.start()
    kept_ref[...] = env_ref[...]
    for copy in copies:
        copy.wait()
    me = lax.axis_index("sec")
    at = place_of(dest_ref[...] ^ me, peers) * vec_ref.shape[1] + slot_ref[...]
    at_ref[...] = jnp.broadcast_to(at[:, :, None], at_ref.shape)
    vecs, secs, width, wide = vec_ref.shape
    low = lax.broadcasted_iota(jnp.int32, (width, wide), 1) % (2 * width) < width

    def turn(x):
        parts = [
            pltpu.roll(x[:, c : c + 2 * width], width, 1) for c in range(0, wide, 2 * width)
        ]
        return jnp.concatenate(parts, 1)

    for a in range(secs):
        turned = left_ref[a].T
        for v in range(vecs):
            both = jnp.dot(turned, vec_ref[v, a], preferred_element_type=jnp.float32).astype(jnp.bfloat16)
            first, second = both[:width], both[width:]
            mixed_ref[a, 0, v * width : (v + 1) * width, :] = jnp.where(low, first, turn(second))
            mixed_ref[a, 1, v * width : (v + 1) * width, :] = jnp.where(low, turn(first), second)


def close_kernel(at_ref, mixed_ref, env_ref, out_ref, done_ref, sems):
    secs, terms, tall, wide = mixed_ref.shape
    width = env_ref.shape[1]
    pairs = wide // width
    vecs = tall // width
    copies = []

    where = at_ref[...]

    def env_at(a, p):
        return env_ref[where[a, p, 0]]

    for a in range(secs):
        for p in range(0, pairs, 2):
            first = env_at(a, p)
            second = env_at(a, p + 1)
            zero = jnp.zeros_like(first)
            top = jnp.concatenate([first, zero], 1)
            bottom = jnp.concatenate([zero, second], 1)
            weights = jnp.concatenate([top, bottom], 0)
            cols = slice(p * width, (p + 2) * width)
            rows = jnp.concatenate([mixed_ref[a, w, :, cols] for w in range(2)], 1)
            block = lax.dot_general(
                rows, weights, (((1,), (1,)), ((), ())), preferred_element_type=jnp.float32
            ).astype(jnp.bfloat16)
            for v in range(vecs):
                done_ref[v, a, :, cols] = block[v * width : (v + 1) * width]
        copy = pltpu.make_async_copy(done_ref.at[:, a], out_ref.at[:, a], sems.at[a])
        copy.start()
        copies.append(copy)
    for copy in copies:
        copy.wait()


def body(vectors, left_env, right_env, target_device, target_slot):
    peers = lax.axis_size("sec")
    vecs, secs, width, wide = vectors.shape
    pairs = wide // width
    terms = left_env.shape[2] // width
    dest = target_device.reshape(secs, pairs)
    bits = bits_of(peers)
    env = right_env
    paired = len(bits) == 3
    if bits:
        far = hop(right_env, bits[0] | 1, peers)
        if paired:
            near = hop(right_env, bits[2] | 1, peers)
        env = jnp.concatenate([right_env, far], 0)
    mixed, kept, at = pl.pallas_call(
        functools.partial(mix_kernel, peers),
        out_shape=(
            jax.ShapeDtypeStruct((secs, terms, vecs * width, wide), jnp.bfloat16),
            jax.ShapeDtypeStruct(env.shape, env.dtype),
            jax.ShapeDtypeStruct((secs, pairs, 128), jnp.int32),
        ),
        in_specs=[pl.BlockSpec(memory_space=pltpu.HBM)] * 4 + [pl.BlockSpec(memory_space=pltpu.VMEM)],
        scratch_shapes=[
            pltpu.VMEM(left_env.shape, jnp.bfloat16),
            pltpu.VMEM(vectors.shape, jnp.bfloat16),
            pltpu.VMEM(dest.shape, jnp.int32),
            pltpu.VMEM(target_slot.shape, jnp.int32),
            pltpu.SemaphoreType.DMA((4,)),
        ],
        compiler_params=pltpu.CompilerParams(vmem_limit_bytes=16 * 2**20),
        cost_estimate=pl.CostEstimate(
            flops=2 * vecs * secs * terms * width * width * wide,
            bytes_accessed=6 * vecs * secs * width * wide,
            transcendentals=0,
        ),
    )(*[pltpu.with_memory_space_constraint(x, pltpu.HBM) for x in (left_env, vectors, dest, target_slot)], env)
    if paired:
        corner = hop(env, (bits[1] ^ bits[2]) | 1, peers)
        side = hop(env, bits[1] | 1, peers)
        rest = hop(far, bits[2] | 1, peers)
        early = jnp.concatenate([near, corner, kept], 0)
        late = jnp.concatenate([rest, side], 0)
        env = jnp.concatenate([early, late, hop(early, 1, peers), hop(late, 1, peers)], 0)
    else:
        for bit in bits[1:]:
            env = kept = jnp.concatenate([kept, hop(env, bit | 1, peers)], 0)
        if peers > 1:
            env = jnp.concatenate([kept, hop(env, 1, peers)], 0)
    return pl.pallas_call(
        close_kernel,
        out_shape=jax.ShapeDtypeStruct(vectors.shape, jnp.bfloat16),
        in_specs=[
            pl.BlockSpec(memory_space=pltpu.VMEM),
            pl.BlockSpec(memory_space=pltpu.VMEM),
            pl.BlockSpec(memory_space=pltpu.VMEM),
        ],
        out_specs=pl.BlockSpec(memory_space=pl.ANY),
        scratch_shapes=[pltpu.VMEM(vectors.shape, jnp.bfloat16), pltpu.SemaphoreType.DMA((secs,))],
        compiler_params=pltpu.CompilerParams(vmem_limit_bytes=16 * 2**20),
        cost_estimate=pl.CostEstimate(
            flops=2 * vecs * secs * terms * width * width * wide,
            bytes_accessed=6 * vecs * secs * width * wide,
            transcendentals=0,
        ),
    )(at, mixed, env)


def solution(mesh):
    return jax.shard_map(
        body,
        mesh=mesh,
        in_specs=(
            P(None, ("grp", "sec"), None, None),
            P(("grp", "sec"), None, None),
            P(("grp", "sec"), None, None),
            P(("grp", "sec"), None, None),
            P(("grp", "sec"), None),
        ),
        out_specs=P(None, ("grp", "sec"), None, None),
        check_vma=False,
    )
```
